32 devices in a mesh: band: 8 (over y, x, core), grid: 4 (over z).
Axes of the slice: x: 2, y: 2, z: 4, core: 2. Of those that a mesh axis runs over, the one named last changes fastest.
Arguments:
- valence: bfloat16 [16, 2, 160, 160, 160], P('band', None, 'grid'), may hold values from -6 to 6
- conduction: bfloat16 [8, 2, 160, 160, 160], P('band', None, 'grid'), may hold values from -6 to 6
- val_energy: float32 [16], replicated, may hold values from -12 to -1
- cond_energy: float32 [8], replicated, may hold values from 1 to 16
- cond_band: int32 [8], P('band'), may hold values from 0 to 7, each once
- owners: int32 [2], replicated, may hold values from 0 to 7
- gvectors: int32 [3, 4096], replicated, may hold values from 0 to 159, as said below
Outputs:
- chi0: float32 [2, 4096, 4096], P(None, 'grid', 'band')
The draws below stay inside these ranges and needn't reach their ends.
Inputs may be any that keep to these rules, and one draw needn't show every extreme that they name: `gvectors`: the G-vectors are distinct; each component, read between -80 and 80, lies within -10 to 10. `owners`: each entry is an index along band. `cond_band`: A permutation of the global conduction band numbers.
All inputs are finite; a program needn't handle non-finite values.
Results may differ from the reference program's by a relative error of at most 0.0092.
Values may be sent and summed in bfloat16 or wider, within the bound.
A program may use at most 192 MiB of HBM per device.

```python
import math
import jax
import jax.numpy as jnp
from jax import lax

NFFT = 160
NGS = 4096
GMAX = 10
VAL_DEV = 2
ROUNDS = 2
VAL = 16
COND = 8
PAIRS = 32
N_BAND = 8


def draw_gvectors(key, part):
    side = 2 * GMAX + 1
    chosen = jax.random.permutation(key, side * side * side)[:NGS].astype(jnp.int32)
    comp_first = chosen // (side * side) - GMAX
    comp_second = chosen // side % side - GMAX
    comp_third = chosen % side - GMAX
    return (jnp.stack([comp_first, comp_second, comp_third]) % NFFT).astype(jnp.int32)


def block_levels(stream_key, dims, pieces, least, largest):
    gain = 1.0
    for dim, parts in pieces:
        draws = jax.random.uniform(jax.random.fold_in(jax.random.fold_in(stream_key, 6), dim), (parts,), jnp.float32, least / len(pieces), largest / len(pieces))
        gain = gain * jnp.repeat(jnp.exp(draws), dims[dim] // parts).reshape((-1,) + (1,) * (len(dims) - 1 - dim))
    return gain


def noise(key, shape, deviation, limit, split=(), held_as=jnp.bfloat16):
    array = deviation * jax.random.normal(key, shape, jnp.float32)
    if split:
        array = array * block_levels(key, shape, split, -0.22, 0.18)
    return jnp.clip(array, -limit, limit).astype(held_as)


def setup_inputs(seed: int = 0) -> dict:
    seeds = jax.random.split(jax.random.key(seed), 8)
    valence = noise(seeds[0], (VAL, 2, NFFT, NFFT, NFFT), 1.0, 6.0, ((0, 8), (2, 4)))
    conduction = noise(seeds[1], (COND, 2, NFFT, NFFT, NFFT), 1.0, 6.0, ((0, 8), (2, 4)))
    val_energy = jnp.clip(jax.random.uniform(seeds[2], (VAL,), jnp.float32, -12.0, -1.0), -12.0, -1.0)
    cond_energy = jnp.clip(jax.random.uniform(seeds[3], (COND,), jnp.float32, 1.0, 16.0), 1.0, 16.0)
    cond_band = jax.random.permutation(seeds[4], COND).astype(jnp.int32)
    owners = jax.random.randint(seeds[5], (ROUNDS,), 0, N_BAND).astype(jnp.int32)
    gvectors = draw_gvectors(jax.random.fold_in(seeds[7], 71), 0)
    return dict(valence=valence, conduction=conduction, val_energy=val_energy, cond_energy=cond_energy, cond_band=cond_band, owners=owners, gvectors=gvectors)


def dft_tables(length):
    positions = jnp.arange(length, dtype=jnp.int32)
    phase_index = (positions[:, None] * positions[None, :]) % length
    angles = phase_index.astype(jnp.float32) * (2.0 * math.pi / length)
    return jnp.cos(angles).astype(jnp.bfloat16), jnp.sin(angles).astype(jnp.bfloat16)


def wide_table(cos_table, sin_table):
    top_half = jnp.concatenate([cos_table, -sin_table], axis=1)
    low_half = jnp.concatenate([sin_table, cos_table], axis=1)
    return jnp.concatenate([top_half, low_half], axis=0)


def plane_transform(density, wide, cos_table, sin_table):
    length = cos_table.shape[0]
    along_z = jnp.einsum("xyk,kq->xyq", density.astype(jnp.float32), wide.astype(jnp.float32)).astype(jnp.bfloat16)
    cos_part = jnp.einsum("xyk,yq->xqk", along_z.astype(jnp.float32), cos_table.astype(jnp.float32))
    sin_part = jnp.einsum("xyk,yq->xqk", along_z.astype(jnp.float32), sin_table.astype(jnp.float32))
    real_part = cos_part[..., :length] + sin_part[..., length:]
    imag_part = cos_part[..., length:] - sin_part[..., :length]
    return jnp.concatenate([real_part, imag_part], axis=-1).astype(jnp.bfloat16)


def pair_matrix(plane, gvectors, cos_table, sin_table):
    length = cos_table.shape[0]
    freq_x, freq_y, freq_z = gvectors[0], gvectors[1], gvectors[2]
    plane_re = plane[:, freq_y, freq_z].astype(jnp.float32)
    plane_im = plane[:, freq_y, freq_z + length].astype(jnp.float32)
    twiddle_cos = cos_table[:, freq_x].astype(jnp.float32)
    twiddle_sin = sin_table[:, freq_x].astype(jnp.float32)
    norm_factor = float(length) ** -1.5
    elem_re = jnp.sum(plane_re * twiddle_cos + plane_im * twiddle_sin, axis=0) * norm_factor
    elem_im = jnp.sum(plane_im * twiddle_cos - plane_re * twiddle_sin, axis=0) * norm_factor
    return jnp.stack([elem_re, elem_im])


def reference(valence, conduction, val_energy, cond_energy, cond_band, owners, gvectors):
    cos_table, sin_table = dft_tables(NFFT)
    wide = wide_table(cos_table, sin_table)
    cond_levels = cond_energy[cond_band]
    elem_list = []
    weight_list = []
    for round_no in range(ROUNDS):
        start = (owners[round_no] * VAL_DEV).astype(jnp.int32)
        round_bands = lax.dynamic_slice_in_dim(valence, start, VAL_DEV, 0)
        val_levels = lax.dynamic_slice_in_dim(val_energy, start, VAL_DEV, 0)
        for band_no in range(VAL_DEV):
            val_wave = round_bands[band_no].astype(jnp.float32)

            def pair_elements(cond_wave):
                cond_f = cond_wave.astype(jnp.float32)
                dens_re = val_wave[0] * cond_f[0] + val_wave[1] * cond_f[1]
                dens_im = val_wave[0] * cond_f[1] - val_wave[1] * cond_f[0]
                density = jnp.concatenate([dens_re, dens_im], axis=-1).astype(jnp.bfloat16)
                plane = plane_transform(density, wide, cos_table, sin_table)
                return pair_matrix(plane, gvectors, cos_table, sin_table)

            elem_list.append(lax.map(pair_elements, conduction))
            weight_list.append(2.0 / (PAIRS * (val_levels[band_no] - cond_levels)))
    elements = jnp.concatenate(elem_list, axis=0)
    weight = jnp.concatenate(weight_list, axis=0)
    weighted = elements * weight[:, None, None]
    high = lax.Precision.HIGHEST
    chi_re = jnp.dot(weighted[:, 0].T, elements[:, 0], precision=high) + jnp.dot(weighted[:, 1].T, elements[:, 1], precision=high)
    chi_im = jnp.dot(weighted[:, 1].T, elements[:, 0], precision=high) - jnp.dot(weighted[:, 0].T, elements[:, 1], precision=high)
    return jnp.stack([chi_re, chi_im])
```

```python
import math

import jax
import jax.numpy as jnp
from jax import lax
from jax.sharding import PartitionSpec as P

ROUNDS = 2
GMAX = 10
SIDE = 2 * GMAX + 1


def from_root(block, axis, owner):
    block = jnp.where(lax.axis_index(axis) == owner, block, jnp.zeros_like(block))
    return lax.psum(block, axis)


def twiddles(freqs, positions, length):
    phase = (freqs * positions) % length
    angles = phase.astype(jnp.float32) * (2.0 * math.pi / length)
    return jnp.cos(angles).astype(jnp.bfloat16), jnp.sin(angles).astype(jnp.bfloat16)


def low_tables(length):
    freqs = (jnp.arange(SIDE, dtype=jnp.int32) - GMAX) % length
    return twiddles(freqs[None, :], jnp.arange(length, dtype=jnp.int32)[:, None], length)


def planes_of(valence, conduction, owners):
    length = valence.shape[3]
    val_dev, x_local = valence.shape[0], valence.shape[2]
    cos_low, sin_low = low_tables(length)
    wide = jnp.concatenate(
        [
            jnp.concatenate([cos_low, -sin_low], axis=1),
            jnp.concatenate([sin_low, cos_low], axis=1),
        ],
        axis=0,
    )
    cond_f = conduction[0].astype(jnp.float32)
    planes = []
    for round_no in range(ROUNDS):
        val_bands = from_root(valence, "band", owners[round_no]).astype(jnp.float32)
        dens_re = val_bands[:, 0] * cond_f[0] + val_bands[:, 1] * cond_f[1]
        dens_im = val_bands[:, 0] * cond_f[1] - val_bands[:, 1] * cond_f[0]
        density = jnp.concatenate([dens_re, dens_im], axis=-1).astype(jnp.bfloat16)
        along_z = jnp.einsum(
            "bxyk,kq->bxyq", density, wide, preferred_element_type=jnp.float32
        ).astype(jnp.bfloat16)
        cos_part = jnp.einsum("bxyk,yq->bxqk", along_z, cos_low, preferred_element_type=jnp.float32)
        sin_part = jnp.einsum("bxyk,yq->bxqk", along_z, sin_low, preferred_element_type=jnp.float32)
        real_part = cos_part[..., :SIDE] + sin_part[..., SIDE:]
        imag_part = cos_part[..., SIDE:] - sin_part[..., :SIDE]
        plane = jnp.stack([real_part, imag_part], axis=1).astype(jnp.bfloat16)
        planes.append(plane.reshape(val_dev, 2, x_local, SIDE * SIDE))
    return jnp.concatenate(planes, axis=0)


def chi_block(plane, gvectors, scale, length):
    grid_pos = lax.axis_index("grid")
    band_pos = lax.axis_index("band")
    pairs, _, x_local, _ = plane.shape
    freq_x, freq_y, freq_z = (gvectors[0], gvectors[1], gvectors[2])
    count = freq_x.shape[0]
    column = (freq_y + GMAX) % length * SIDE + (freq_z + GMAX) % length
    chosen = (jnp.arange(SIDE * SIDE, dtype=jnp.int32)[:, None] == column[None, :]).astype(jnp.bfloat16)
    at_g = jnp.dot(
        plane.reshape(pairs * 2 * x_local, SIDE * SIDE), chosen, preferred_element_type=jnp.float32
    ).reshape(pairs, 2, x_local, count)
    positions = grid_pos * x_local + jnp.arange(x_local, dtype=jnp.int32)
    cos_g, sin_g = twiddles(freq_x[None, :], positions[:, None], length)
    cos_g, sin_g = cos_g.astype(jnp.float32), sin_g.astype(jnp.float32)
    elem_re = jnp.sum(at_g[:, 0] * cos_g + at_g[:, 1] * sin_g, axis=1)
    elem_im = jnp.sum(at_g[:, 1] * cos_g - at_g[:, 0] * sin_g, axis=1)
    local = jnp.stack([elem_re, elem_im], axis=1) * scale[:, None, None]
    summed = lax.psum(local, "grid")
    gathered = lax.all_gather(summed, "band", axis=0, tiled=True)
    row_count = count // lax.axis_size("grid")
    col_count = count // lax.axis_size("band")
    rows = lax.dynamic_slice_in_dim(gathered, grid_pos * row_count, row_count, 2)
    cols = lax.dynamic_slice_in_dim(gathered, band_pos * col_count, col_count, 2)
    right_side = jnp.concatenate([cols[:, 0], cols[:, 1]], axis=0)
    left_real = jnp.concatenate([-rows[:, 0], -rows[:, 1]], axis=0)
    left_imag = jnp.concatenate([-rows[:, 1], rows[:, 0]], axis=0)
    high = lax.Precision.HIGHEST
    chi_re = jnp.einsum("pr,pc->rc", left_real, right_side, precision=high)
    chi_im = jnp.einsum("pr,pc->rc", left_imag, right_side, precision=high)
    return jnp.stack([chi_re, chi_im])


def pair_scale(val_energy, cond_energy, cond_band, owners, val_dev, length):
    pairs_all = ROUNDS * val_dev * cond_band.shape[0] * lax.axis_size("band")
    cond_numbers = jnp.arange(cond_energy.shape[0], dtype=jnp.int32)
    cond_level = jnp.sum(jnp.where(cond_band[0] == cond_numbers, cond_energy, 0.0))
    val_numbers = (owners[:, None] * val_dev + jnp.arange(val_dev, dtype=jnp.int32)[None]).reshape(-1)
    which = val_numbers[:, None] == jnp.arange(val_energy.shape[0], dtype=jnp.int32)[None]
    val_levels = jnp.sum(jnp.where(which, val_energy[None], 0.0), axis=1)
    return jnp.sqrt(2.0 / (pairs_all * (cond_level - val_levels))) * float(length) ** (-1.5)


def shards(valence, conduction, val_energy, cond_energy, cond_band, owners, gvectors):
    length = valence.shape[3]
    plane = planes_of(valence, conduction, owners)
    scale = pair_scale(val_energy, cond_energy, cond_band, owners, valence.shape[0], length)
    return chi_block(plane, gvectors, scale, length)


def solution(mesh):
    return jax.shard_map(
        shards,
        mesh=mesh,
        in_specs=(
            P("band", None, "grid", None, None),
            P("band", None, "grid", None, None),
            P(),
            P(),
            P("band"),
            P(),
            P(),
        ),
        out_specs=P(None, "grid", "band"),
        check_vma=False,
    )
```

```python
import functools
import math

import jax
import jax.numpy as jnp
import numpy as np
from jax import lax
from jax.experimental import pallas as pl
from jax.experimental.pallas import tpu as pltpu
from jax.sharding import PartitionSpec as P

ROUNDS = 2
GMAX = 10
SIDE = 2 * GMAX + 1


def twiddles(freqs, positions, length):
    phase = (freqs * positions) % length
    angles = phase.astype(jnp.float32) * (2.0 * math.pi / length)
    return jnp.cos(angles).astype(jnp.bfloat16), jnp.sin(angles).astype(jnp.bfloat16)


MESH = pl.DeviceIdType.MESH
LANES = 128
PACK = 4
KPAD = 32
ROWS = 32


def low_numpy(length):
    freqs = np.arange(SIDE) - GMAX
    angles = (np.arange(length)[:, None] * freqs[None, :]) % length * (2.0 * math.pi / length)
    pad = ((0, 0), (0, KPAD - SIDE))
    return np.pad(np.cos(angles), pad), np.pad(np.sin(angles), pad)


def z_table(length):
    cos_low, sin_low = low_numpy(length)
    tail = length - LANES

    def spread(table):
        out = np.zeros((PACK + 1, LANES, PACK, KPAD))
        for i in range(PACK):
            out[i, :, i] = table[:LANES]
            out[PACK, i * tail : (i + 1) * tail, i] = table[LANES:]
        return out.reshape(PACK + 1, LANES, PACK * KPAD)

    cos_wide, sin_wide = spread(cos_low), spread(sin_low)
    top = np.concatenate([cos_wide, -sin_wide], axis=2)
    low = np.concatenate([sin_wide, cos_wide], axis=2)
    return jnp.asarray(np.concatenate([top, low], axis=1), jnp.float32).astype(jnp.bfloat16)


def y_table(length):
    cos_low, sin_low = low_numpy(length)
    return jnp.asarray(np.concatenate([cos_low, sin_low], axis=1).T, jnp.float32).astype(jnp.bfloat16)


def pack_kernel(in_ref, out_ref):
    bands = in_ref.shape[0]
    length = in_ref.shape[3]
    for band in range(bands):
        for comp in range(2):
            tails = []
            for i in range(PACK):
                whole = in_ref[band, comp, i]
                for block in range(length // ROWS):
                    out_ref[band, block, comp, i] = whole[block * ROWS : (block + 1) * ROWS, :LANES]
                tails.append(whole[:, LANES:])
            tail = jnp.concatenate(tails, axis=1)
            for block in range(length // ROWS):
                out_ref[band, block, comp, PACK] = tail[block * ROWS : (block + 1) * ROWS]


def packed(wave):
    bands, _, x_local, length, _ = wave.shape
    blocks = length // ROWS
    groups = x_local // PACK
    return pl.pallas_call(
        pack_kernel,
        grid=(groups,),
        out_shape=jax.ShapeDtypeStruct(
            (bands, groups * blocks, 2, PACK + 1, ROWS, LANES), jnp.bfloat16
        ),
        in_specs=[pl.BlockSpec((bands, 2, PACK, length, length), lambda g: (0, 0, g, 0, 0))],
        out_specs=pl.BlockSpec(
            (bands, blocks, 2, PACK + 1, ROWS, LANES), lambda g: (0, g, 0, 0, 0, 0)
        ),
        compiler_params=pltpu.CompilerParams(vmem_limit_bytes=32 * 2**20),
    )(wave)


def to_gray(position, bits):
    index = 0
    for bit in range(bits):
        here = position // 2**bit % 2
        above = position // 2 ** (bit + 1) % 2
        index = index + (here + above) % 2 * 2**bit
    return index


def from_gray(index, bits):
    position = 0
    last = 0
    for bit in reversed(range(bits)):
        last = (last + index // 2**bit % 2) % 2
        position = position + last * 2**bit
    return position


def ring_kernel(
    count, info_ref, val_ref, cond_ref, wz_ref, wy_ref, out_ref, buf, along_z, send_sem, recv_sem
):
    bits = count.bit_length() - 1
    slots = count + 1
    chunks = val_ref.shape[1]
    me = lax.axis_index("band")
    position = from_gray(me, bits)
    after = to_gray((position + 1) % count, bits)
    before = to_gray((position + count - 1) % count, bits)
    targets = (after, before)
    starts = (position, count - 1 - position)
    last = chunks + count - 2

    barrier = pltpu.get_barrier_semaphore()
    for neighbour in targets:
        pl.semaphore_signal(barrier, inc=1, device_id={"band": neighbour}, device_id_type=MESH)
    pl.semaphore_wait(barrier, 2)

    streams = [(r, d) for r in range(ROUNDS) for d in range(2)]

    def copy_of(stream, step):
        now, later = step % slots, (step + 1) % slots
        return pltpu.make_async_remote_copy(
            src_ref=buf.at[stream, now],
            dst_ref=buf.at[stream, later],
            send_sem=send_sem.at[stream, step % 2],
            recv_sem=recv_sem.at[stream, later],
            device_id={"band": targets[stream % 2]},
            device_id_type=MESH,
        )

    def step_body(step, carry):
        now = step % slots
        chunk = [(step + chunks - start) % chunks for start in starts]
        for stream, (r, d) in enumerate(streams):
            @pl.when(step > 0)
            def _():
                copy_of(stream, step + slots - 1).wait_recv()

            own = jnp.logical_or(info_ref[stream] == 1, step == 0)
            buf[stream, now] = jnp.where(own, val_ref[d, chunk[d]], buf[stream, now])

            @pl.when(step < last)
            def _():
                copy_of(stream, step).start()

        for stream in range(len(streams)):
            @pl.when(step > 0)
            def _():
                copy_of(stream, step - 1).wait_send()

        @pl.when(step >= count - 1)
        def _():
            held = [(chunk[d] + info_ref[len(streams) + i]) % chunks for i, (r, d) in enumerate(streams)]
            cond = [cond_ref[0, index].astype(jnp.float32) for index in held]
            total = None
            for j in range(PACK + 1):
                parts = []
                for stream, (r, d) in enumerate(streams):
                    v_re = buf[stream, now, 0, j].astype(jnp.float32)
                    v_im = buf[stream, now, 1, j].astype(jnp.float32)
                    c_re, c_im = cond[stream][0, j], cond[stream][1, j]
                    d_re = (v_re * c_re + v_im * c_im).astype(jnp.bfloat16)
                    d_im = (v_re * c_im - v_im * c_re).astype(jnp.bfloat16)
                    parts.append(jnp.concatenate([d_re, d_im], axis=1))
                term = jnp.dot(
                    jnp.concatenate(parts, axis=0), wz_ref[j], preferred_element_type=jnp.float32
                )
                total = term if total is None else total + term
            rounded = total.astype(jnp.bfloat16)
            for stream, (r, d) in enumerate(streams):
                along_z[stream, chunk[d]] = rounded[stream * ROWS : (stream + 1) * ROWS]

        return carry

    lax.fori_loop(0, last + 1, step_body, 0)

    groups = out_ref.shape[1]
    blocks = chunks // groups

    def group_body(group, carry):
        for stream in range(len(streams)):
            first = group * blocks + chunks - info_ref[len(streams) + stream]
            block = jnp.concatenate(
                [along_z[stream, (first + b) % chunks] for b in range(blocks)], axis=0
            )
            both = jnp.dot(wy_ref[...], block, preferred_element_type=jnp.float32)
            cos_part, sin_part = both[:KPAD], both[KPAD:]
            real = cos_part[:, :LANES] + sin_part[:, LANES:]
            imag = cos_part[:, LANES:] - sin_part[:, :LANES]
            out_ref[stream, group, 0] = real.astype(jnp.bfloat16)
            out_ref[stream, group, 1] = imag.astype(jnp.bfloat16)
        return carry

    lax.fori_loop(0, groups, group_body, 0)


def planes_of(valence, conduction, owners):
    val_dev, _, x_local, length, _ = valence.shape
    groups = x_local // PACK
    count = lax.axis_size("band")
    streams = ROUNDS * val_dev
    chunk = (2, PACK + 1, ROWS, LANES)
    vmem = pl.BlockSpec(memory_space=pltpu.VMEM)
    chunks = groups * (length // ROWS)
    bits = count.bit_length() - 1
    me = lax.axis_index("band")
    behind = from_gray(me, bits) - from_gray(owners, bits)
    shift = jnp.where(jnp.stack([behind < 0, behind > 0], axis=1), chunks - count, 0)
    is_owner = jnp.broadcast_to((owners == me)[:, None], (ROUNDS, val_dev))
    info = jnp.concatenate([is_owner.reshape(-1).astype(jnp.int32), shift.reshape(-1).astype(jnp.int32)])
    plane = pl.pallas_call(
        functools.partial(ring_kernel, count),
        out_shape=jax.ShapeDtypeStruct((streams, groups, 2, KPAD, LANES), jnp.bfloat16),
        in_specs=[pl.BlockSpec(memory_space=pltpu.SMEM), vmem, vmem, vmem, vmem],
        out_specs=vmem,
        scratch_shapes=[
            pltpu.VMEM((streams, count + 1) + chunk, jnp.bfloat16),
            pltpu.VMEM((streams, chunks, ROWS, 2 * LANES), jnp.bfloat16),
            pltpu.SemaphoreType.DMA((streams, 2)),
            pltpu.SemaphoreType.DMA((streams, count + 1)),
        ],
        compiler_params=pltpu.CompilerParams(
            collective_id=0, has_side_effects=True, vmem_limit_bytes=48 * 2**20
        ),
        cost_estimate=pl.CostEstimate(
            flops=streams * chunks * ROWS * 1280 * 512, bytes_accessed=2 * valence.size, transcendentals=0
        ),
    )(info, packed(valence), packed(conduction), z_table(length), y_table(length))
    plane = plane.reshape(streams, groups, 2, KPAD, PACK, KPAD)[:, :, :, :SIDE, :, :SIDE]
    return plane.transpose(0, 2, 1, 4, 3, 5).reshape(streams, 2, x_local, SIDE * SIDE)


def chi_block(plane, gvectors, scale, length):
    grid_pos = lax.axis_index("grid")
    band_pos = lax.axis_index("band")
    pairs, _, x_local, _ = plane.shape
    freq_x, freq_y, freq_z = (gvectors[0], gvectors[1], gvectors[2])
    count = freq_x.shape[0]
    column = (freq_y + GMAX) % length * SIDE + (freq_z + GMAX) % length
    chosen = (jnp.arange(SIDE * SIDE, dtype=jnp.int32)[:, None] == column[None, :]).astype(jnp.bfloat16)
    at_g = jnp.dot(
        plane.reshape(pairs * 2 * x_local, SIDE * SIDE), chosen, preferred_element_type=jnp.float32
    ).reshape(pairs, 2, x_local, count)
    positions = grid_pos * x_local + jnp.arange(x_local, dtype=jnp.int32)
    cos_g, sin_g = twiddles(freq_x[None, :], positions[:, None], length)
    cos_g, sin_g = cos_g.astype(jnp.float32), sin_g.astype(jnp.float32)
    elem_re = jnp.sum(at_g[:, 0] * cos_g + at_g[:, 1] * sin_g, axis=1)
    elem_im = jnp.sum(at_g[:, 1] * cos_g - at_g[:, 0] * sin_g, axis=1)
    local = jnp.stack([elem_re, elem_im], axis=1) * scale[:, None, None]
    summed = lax.psum(local, "grid")
    gathered = lax.all_gather(summed, "band", axis=0, tiled=True)
    row_count = count // lax.axis_size("grid")
    col_count = count // lax.axis_size("band")
    rows = lax.dynamic_slice_in_dim(gathered, grid_pos * row_count, row_count, 2)
    cols = lax.dynamic_slice_in_dim(gathered, band_pos * col_count, col_count, 2)
    right_side = jnp.concatenate([cols[:, 0], cols[:, 1]], axis=0)
    left_real = jnp.concatenate([-rows[:, 0], -rows[:, 1]], axis=0)
    left_imag = jnp.concatenate([-rows[:, 1], rows[:, 0]], axis=0)
    high = lax.Precision.HIGHEST
    chi_re = jnp.einsum("pr,pc->rc", left_real, right_side, precision=high)
    chi_im = jnp.einsum("pr,pc->rc", left_imag, right_side, precision=high)
    return jnp.stack([chi_re, chi_im])


def pair_scale(val_energy, cond_energy, cond_band, owners, val_dev, length):
    pairs_all = ROUNDS * val_dev * cond_band.shape[0] * lax.axis_size("band")
    cond_numbers = jnp.arange(cond_energy.shape[0], dtype=jnp.int32)
    cond_level = jnp.sum(jnp.where(cond_band[0] == cond_numbers, cond_energy, 0.0))
    val_numbers = (owners[:, None] * val_dev + jnp.arange(val_dev, dtype=jnp.int32)[None]).reshape(-1)
    which = val_numbers[:, None] == jnp.arange(val_energy.shape[0], dtype=jnp.int32)[None]
    val_levels = jnp.sum(jnp.where(which, val_energy[None], 0.0), axis=1)
    return jnp.sqrt(2.0 / (pairs_all * (cond_level - val_levels))) * float(length) ** (-1.5)


def shards(valence, conduction, val_energy, cond_energy, cond_band, owners, gvectors):
    length = valence.shape[3]
    plane = planes_of(valence, conduction, owners)
    scale = pair_scale(val_energy, cond_energy, cond_band, owners, valence.shape[0], length)
    return chi_block(plane, gvectors, scale, length)


def solution(mesh):
    return jax.shard_map(
        shards,
        mesh=mesh,
        in_specs=(
            P("band", None, "grid", None, None),
            P("band", None, "grid", None, None),
            P(),
            P(),
            P("band"),
            P(),
            P(),
        ),
        out_specs=P(None, "grid", "band"),
        check_vma=False,
    )
```

```python
import functools
import math

import jax
import jax.numpy as jnp
import numpy as np
from jax import lax
from jax.experimental import pallas as pl
from jax.experimental.pallas import tpu as pltpu
from jax.sharding import PartitionSpec as P

ROUNDS = 2
GMAX = 10
SIDE = 2 * GMAX + 1


def twiddles(freqs, positions, length):
    phase = (freqs * positions) % length
    angles = phase.astype(jnp.float32) * (2.0 * math.pi / length)
    return jnp.cos(angles).astype(jnp.bfloat16), jnp.sin(angles).astype(jnp.bfloat16)


MESH = pl.DeviceIdType.MESH
LANES = 128
PACK = 4
KPAD = 32
ROWS = 80


def low_numpy(length):
    freqs = np.arange(SIDE) - GMAX
    angles = (np.arange(length)[:, None] * freqs[None, :]) % length * (2.0 * math.pi / length)
    pad = ((0, 0), (0, KPAD - SIDE))
    return np.pad(np.cos(angles), pad), np.pad(np.sin(angles), pad)


def z_table(length):
    cos_low, sin_low = low_numpy(length)
    tail = length - LANES

    def spread(table):
        out = np.zeros((PACK + 1, LANES, PACK, KPAD))
        for i in range(PACK):
            out[i, :, i] = table[:LANES]
            out[PACK, i * tail : (i + 1) * tail, i] = table[LANES:]
        return out.reshape(PACK + 1, LANES, PACK * KPAD)

    cos_wide, sin_wide = spread(cos_low), spread(sin_low)
    top = np.concatenate([cos_wide, -sin_wide], axis=2)
    low = np.concatenate([sin_wide, cos_wide], axis=2)
    return jnp.asarray(np.concatenate([top, low], axis=1), jnp.float32).astype(jnp.bfloat16)


def y_table(length):
    cos_low, sin_low = low_numpy(length)
    return jnp.asarray(np.concatenate([cos_low, sin_low], axis=1).T, jnp.float32).astype(jnp.bfloat16)


def pack_kernel(in_ref, out_ref):
    bands = in_ref.shape[0]
    length = in_ref.shape[3]
    for band in range(bands):
        for comp in range(2):
            tails = []
            for i in range(PACK):
                whole = in_ref[band, comp, i]
                for block in range(length // ROWS):
                    out_ref[band, block, comp, i] = whole[block * ROWS : (block + 1) * ROWS, :LANES]
                tails.append(whole[:, LANES:])
            tail = jnp.concatenate(tails, axis=1)
            for block in range(length // ROWS):
                out_ref[band, block, comp, PACK] = tail[block * ROWS : (block + 1) * ROWS]


def packed(wave):
    bands, _, x_local, length, _ = wave.shape
    blocks = length // ROWS
    groups = x_local // PACK
    return pl.pallas_call(
        pack_kernel,
        grid=(groups,),
        out_shape=jax.ShapeDtypeStruct(
            (bands, groups * blocks, 2, PACK + 1, ROWS, LANES), jnp.bfloat16
        ),
        in_specs=[pl.BlockSpec((bands, 2, PACK, length, length), lambda g: (0, 0, g, 0, 0))],
        out_specs=pl.BlockSpec(
            (bands, blocks, 2, PACK + 1, ROWS, LANES), lambda g: (0, g, 0, 0, 0, 0)
        ),
        compiler_params=pltpu.CompilerParams(vmem_limit_bytes=32 * 2**20),
    )(wave)


def to_gray(position, bits):
    index = 0
    for bit in range(bits):
        here = position // 2**bit % 2
        above = position // 2 ** (bit + 1) % 2
        index = index + (here + above) % 2 * 2**bit
    return index


def from_gray(index, bits):
    position = 0
    last = 0
    for bit in reversed(range(bits)):
        last = (last + index // 2**bit % 2) % 2
        position = position + last * 2**bit
    return position


def ring_kernel(
    count, info_ref, val_ref, cond_ref, wz_ref, wy_ref, out_ref, buf, along_z, send_sem, recv_sem
):
    bits = count.bit_length() - 1
    slots = count + 1
    chunks = val_ref.shape[1]
    me = lax.axis_index("band")
    position = from_gray(me, bits)
    after = to_gray((position + 1) % count, bits)
    before = to_gray((position + count - 1) % count, bits)
    targets = (after, before)
    starts = (position, count - 1 - position)
    last = chunks + count - 2

    barrier = pltpu.get_barrier_semaphore()
    for neighbour in targets:
        pl.semaphore_signal(barrier, inc=1, device_id={"band": neighbour}, device_id_type=MESH)
    pl.semaphore_wait(barrier, 2)

    streams = [(r, d) for r in range(ROUNDS) for d in range(2)]

    def copy_of(stream, step):
        now, later = step % slots, (step + 1) % slots
        return pltpu.make_async_remote_copy(
            src_ref=buf.at[stream, now],
            dst_ref=buf.at[stream, later],
            send_sem=send_sem.at[stream, step % 2],
            recv_sem=recv_sem.at[stream, later],
            device_id={"band": targets[stream % 2]},
            device_id_type=MESH,
        )

    def step_body(step, carry):
        now = step % slots
        chunk = [(step + chunks - start) % chunks for start in starts]
        for stream, (r, d) in enumerate(streams):
            @pl.when(step > 0)
            def _():
                copy_of(stream, step + slots - 1).wait_recv()

            own = jnp.logical_or(info_ref[stream] == 1, step == 0)
            buf[stream, now] = jnp.where(own, val_ref[d, chunk[d]], buf[stream, now])

            @pl.when(step < last)
            def _():
                copy_of(stream, step).start()

        for stream in range(len(streams)):
            @pl.when(step > 0)
            def _():
                copy_of(stream, step - 1).wait_send()

        @pl.when(step >= count - 1)
        def _():
            held = [(chunk[d] + info_ref[len(streams) + i]) % chunks for i, (r, d) in enumerate(streams)]
            cond = [cond_ref[0, index].astype(jnp.float32) for index in held]
            total = None
            for j in range(PACK + 1):
                parts = []
                for stream, (r, d) in enumerate(streams):
                    v_re = buf[stream, now, 0, j].astype(jnp.float32)
                    v_im = buf[stream, now, 1, j].astype(jnp.float32)
                    c_re, c_im = cond[stream][0, j], cond[stream][1, j]
                    d_re = (v_re * c_re + v_im * c_im).astype(jnp.bfloat16)
                    d_im = (v_re * c_im - v_im * c_re).astype(jnp.bfloat16)
                    parts.append(jnp.concatenate([d_re, d_im], axis=1))
                term = jnp.dot(
                    jnp.concatenate(parts, axis=0), wz_ref[j], preferred_element_type=jnp.float32
                )
                total = term if total is None else total + term
            rounded = total.astype(jnp.bfloat16)
            for stream, (r, d) in enumerate(streams):
                along_z[stream, chunk[d]] = rounded[stream * ROWS : (stream + 1) * ROWS]

        return carry

    lax.fori_loop(0, last + 1, step_body, 0)

    groups = out_ref.shape[1]
    blocks = chunks // groups

    def group_body(group, carry):
        for stream in range(len(streams)):
            first = group * blocks + chunks - info_ref[len(streams) + stream]
            block = jnp.concatenate(
                [along_z[stream, (first + b) % chunks] for b in range(blocks)], axis=0
            )
            both = jnp.dot(wy_ref[...], block, preferred_element_type=jnp.float32)
            cos_part, sin_part = both[:KPAD], both[KPAD:]
            real = cos_part[:, :LANES] + sin_part[:, LANES:]
            imag = cos_part[:, LANES:] - sin_part[:, :LANES]
            out_ref[stream, group, 0] = real.astype(jnp.bfloat16)
            out_ref[stream, group, 1] = imag.astype(jnp.bfloat16)
        return carry

    lax.fori_loop(0, groups, group_body, 0)


def planes_of(valence, conduction, owners):
    val_dev, _, x_local, length, _ = valence.shape
    groups = x_local // PACK
    count = lax.axis_size("band")
    streams = ROUNDS * val_dev
    chunk = (2, PACK + 1, ROWS, LANES)
    vmem = pl.BlockSpec(memory_space=pltpu.VMEM)
    chunks = groups * (length // ROWS)
    bits = count.bit_length() - 1
    me = lax.axis_index("band")
    behind = from_gray(me, bits) - from_gray(owners, bits)
    shift = jnp.where(jnp.stack([behind < 0, behind > 0], axis=1), chunks - count, 0)
    is_owner = jnp.broadcast_to((owners == me)[:, None], (ROUNDS, val_dev))
    info = jnp.concatenate([is_owner.reshape(-1).astype(jnp.int32), shift.reshape(-1).astype(jnp.int32)])
    plane = pl.pallas_call(
        functools.partial(ring_kernel, count),
        out_shape=jax.ShapeDtypeStruct((streams, groups, 2, KPAD, LANES), jnp.bfloat16),
        in_specs=[pl.BlockSpec(memory_space=pltpu.SMEM), vmem, vmem, vmem, vmem],
        out_specs=vmem,
        scratch_shapes=[
            pltpu.VMEM((streams, count + 1) + chunk, jnp.bfloat16),
            pltpu.VMEM((streams, chunks, ROWS, 2 * LANES), jnp.bfloat16),
            pltpu.SemaphoreType.DMA((streams, 2)),
            pltpu.SemaphoreType.DMA((streams, count + 1)),
        ],
        compiler_params=pltpu.CompilerParams(
            collective_id=0, has_side_effects=True, vmem_limit_bytes=48 * 2**20
        ),
        cost_estimate=pl.CostEstimate(
            flops=streams * chunks * ROWS * 1280 * 512, bytes_accessed=2 * valence.size, transcendentals=0
        ),
    )(info, packed(valence), packed(conduction), z_table(length), y_table(length))
    plane = plane.reshape(streams, groups, 2, KPAD, PACK, KPAD)[:, :, :, :SIDE, :, :SIDE]
    return plane.transpose(0, 2, 1, 4, 3, 5).reshape(streams, 2, x_local, SIDE * SIDE)


def spread_kernel(
    bands, grids, local_ref, rows_ref, cols_ref, parts, total, part_send, part_recv, row_send, row_recv, col_send, col_recv
):
    band = lax.axis_index("band")
    grid = lax.axis_index("grid")
    ratio = bands // grids
    col_count = cols_ref.shape[2]
    source = band // ratio
    in_own = source == grid

    barrier = pltpu.get_barrier_semaphore()

    def greet(to_band, to_grid):
        pl.semaphore_signal(
            barrier, inc=1, device_id={"band": to_band, "grid": to_grid}, device_id_type=MESH
        )

    for j in range(1, grids):
        greet(band, (grid + j) % grids)
    for j in range(1, bands):
        greet((band + j) % bands, grid)
    for b in range(bands):
        @pl.when(jnp.logical_not(jnp.logical_and(in_own, b == band)))
        def _():
            greet(b, source)
    pl.semaphore_wait(
        barrier, grids - 1 + bands - 1 + bands - jnp.where(in_own, 1, 0).astype(jnp.int32)
    )

    def part_copy(j):
        peer = (grid + j) % grids
        return pltpu.make_async_remote_copy(
            src_ref=local_ref.at[peer],
            dst_ref=parts.at[j],
            send_sem=part_send.at[j],
            recv_sem=part_recv.at[j],
            device_id={"band": band, "grid": peer},
            device_id_type=MESH,
        )

    def row_copy(j):
        return pltpu.make_async_remote_copy(
            src_ref=total,
            dst_ref=rows_ref.at[band],
            send_sem=row_send.at[j],
            recv_sem=row_recv.at[j],
            device_id={"band": (band + j) % bands, "grid": grid},
            device_id_type=MESH,
        )

    def col_copy(q, g):
        return pltpu.make_async_remote_copy(
            src_ref=total.at[:, pl.ds(q * col_count, col_count)],
            dst_ref=cols_ref.at[band],
            send_sem=col_send.at[q * grids + g],
            recv_sem=col_recv.at[band],
            device_id={"band": grid * ratio + q, "grid": g},
            device_id_type=MESH,
        )

    def is_me(q, g):
        return jnp.logical_and(grid * ratio + q == band, grid == g)

    for j in range(1, grids):
        part_copy(j).start()
    summed = local_ref[grid]
    for j in range(1, grids):
        part_copy(j).wait_recv()
        summed = summed + parts[j]
    total[...] = summed
    for q in range(ratio):
        for g in range(grids):
            @pl.when(jnp.logical_not(is_me(q, g)))
            def _():
                col_copy(q, g).start()
    for j in range(1, bands):
        row_copy(j).start()
    rows_ref[band] = summed
    for q in range(ratio):
        @pl.when(is_me(q, grid))
        def _():
            cols_ref[band] = summed[:, q * col_count : (q + 1) * col_count]

    for j in range(1, bands):
        pltpu.make_async_remote_copy(
            src_ref=total,
            dst_ref=rows_ref.at[(band + bands - j) % bands],
            send_sem=row_send.at[j],
            recv_sem=row_recv.at[j],
            device_id={"band": (band + j) % bands, "grid": grid},
            device_id_type=MESH,
        ).wait_recv()
    for b in range(bands):
        @pl.when(jnp.logical_not(jnp.logical_and(in_own, b == band)))
        def _():
            pltpu.make_async_remote_copy(
                src_ref=total.at[:, pl.ds(0, col_count)],
                dst_ref=cols_ref.at[b],
                send_sem=col_send.at[0],
                recv_sem=col_recv.at[b],
                device_id={"band": b, "grid": source},
                device_id_type=MESH,
            ).wait_recv()
    for j in range(1, grids):
        part_copy(j).wait_send()
    for j in range(1, bands):
        row_copy(j).wait_send()
    for q in range(ratio):
        for g in range(grids):
            @pl.when(jnp.logical_not(is_me(q, g)))
            def _():
                col_copy(q, g).wait_send()


def spread(local):
    bands, grids = lax.axis_size("band"), lax.axis_size("grid")
    lines, count = local.shape
    row_count, col_count = count // grids, count // bands
    by_grid = local.reshape(lines, grids, row_count).transpose(1, 0, 2)
    vmem = pl.BlockSpec(memory_space=pltpu.VMEM)
    dma = pltpu.SemaphoreType.DMA
    return pl.pallas_call(
        functools.partial(spread_kernel, bands, grids),
        out_shape=(
            jax.ShapeDtypeStruct((bands, lines, row_count), jnp.float32),
            jax.ShapeDtypeStruct((bands, lines, col_count), jnp.float32),
        ),
        in_specs=[vmem],
        out_specs=(vmem, vmem),
        scratch_shapes=[
            pltpu.VMEM((grids, lines, row_count), jnp.float32),
            pltpu.VMEM((lines, row_count), jnp.float32),
            dma((grids,)),
            dma((grids,)),
            dma((bands,)),
            dma((bands,)),
            dma((bands,)),
            dma((bands,)),
        ],
        compiler_params=pltpu.CompilerParams(
            collective_id=1, has_side_effects=True, vmem_limit_bytes=32 * 2**20
        ),
    )(by_grid)


def chi_block(plane, gvectors, scale, length):
    grid_pos = lax.axis_index("grid")
    pairs, _, x_local, _ = plane.shape
    freq_x, freq_y, freq_z = (gvectors[0], gvectors[1], gvectors[2])
    count = freq_x.shape[0]
    column = (freq_y + GMAX) % length * SIDE + (freq_z + GMAX) % length
    chosen = (jnp.arange(SIDE * SIDE, dtype=jnp.int32)[:, None] == column[None, :]).astype(jnp.bfloat16)
    at_g = jnp.dot(
        plane.reshape(pairs * 2 * x_local, SIDE * SIDE), chosen, preferred_element_type=jnp.float32
    ).reshape(pairs, 2, x_local, count)
    positions = grid_pos * x_local + jnp.arange(x_local, dtype=jnp.int32)
    cos_g, sin_g = twiddles(freq_x[None, :], positions[:, None], length)
    cos_g, sin_g = cos_g.astype(jnp.float32), sin_g.astype(jnp.float32)
    elem_re = jnp.sum(at_g[:, 0] * cos_g + at_g[:, 1] * sin_g, axis=1)
    elem_im = jnp.sum(at_g[:, 1] * cos_g - at_g[:, 0] * sin_g, axis=1)
    local = jnp.stack([elem_re, elem_im], axis=1) * scale[:, None, None]
    bands = lax.axis_size("band")
    rows, cols = spread(local.reshape(pairs * 2, count))
    rows = rows.reshape(bands * pairs, 2, -1)
    cols = cols.reshape(bands * pairs, 2, -1)
    right_side = jnp.concatenate([cols[:, 0], cols[:, 1]], axis=0)
    left_real = jnp.concatenate([-rows[:, 0], -rows[:, 1]], axis=0)
    left_imag = jnp.concatenate([-rows[:, 1], rows[:, 0]], axis=0)
    high = lax.Precision.HIGHEST
    chi_re = jnp.einsum("pr,pc->rc", left_real, right_side, precision=high)
    chi_im = jnp.einsum("pr,pc->rc", left_imag, right_side, precision=high)
    return jnp.stack([chi_re, chi_im])


def pair_scale(val_energy, cond_energy, cond_band, owners, val_dev, length):
    pairs_all = ROUNDS * val_dev * cond_band.shape[0] * lax.axis_size("band")
    cond_numbers = jnp.arange(cond_energy.shape[0], dtype=jnp.int32)
    cond_level = jnp.sum(jnp.where(cond_band[0] == cond_numbers, cond_energy, 0.0))
    val_numbers = (owners[:, None] * val_dev + jnp.arange(val_dev, dtype=jnp.int32)[None]).reshape(-1)
    which = val_numbers[:, None] == jnp.arange(val_energy.shape[0], dtype=jnp.int32)[None]
    val_levels = jnp.sum(jnp.where(which, val_energy[None], 0.0), axis=1)
    return jnp.sqrt(2.0 / (pairs_all * (cond_level - val_levels))) * float(length) ** (-1.5)


def shards(valence, conduction, val_energy, cond_energy, cond_band, owners, gvectors):
    length = valence.shape[3]
    plane = planes_of(valence, conduction, owners)
    scale = pair_scale(val_energy, cond_energy, cond_band, owners, valence.shape[0], length)
    return chi_block(plane, gvectors, scale, length)


def solution(mesh):
    return jax.shard_map(
        shards,
        mesh=mesh,
        in_specs=(
            P("band", None, "grid", None, None),
            P("band", None, "grid", None, None),
            P(),
            P(),
            P("band"),
            P(),
            P(),
        ),
        out_specs=P(None, "grid", "band"),
        check_vma=False,
    )
```
